32 devices in a mesh: grow: 4 (over y, x), gcol: 8 (over z, core).
Axes of the slice: x: 2, y: 2, z: 4, core: 2. Of those that a mesh axis runs over, the one named last changes fastest.
Arguments:
- screened: bfloat16 [2, 16384, 16384], P(None, 'grow', 'gcol'), may hold values from -6 to 6
- elements: bfloat16 [2, 1024, 16384], P(None, None, ('grow', 'gcol')), may hold values from -0.046875 to 0.046875
- energy_grid: float32 [256], replicated, may hold values from -3 to 3
- band_index: int32 [256], replicated, may hold values from 0 to 255
- energy_index: int32 [4, 16], replicated, may hold values from 0 to 255
Outputs:
- sigma: float32 [2, 4, 16], replicated
The draws below stay inside these ranges and needn't reach their ends.
All inputs are finite; a program needn't handle non-finite values.
Results may differ from the reference program's by a relative error of at most 0.0003.
Values may be sent and summed in bfloat16 or wider, within the bound.
A program may use at most 192 MiB of HBM per device.

```python
import jax
import jax.numpy as jnp
from jax import lax

NG = 16384
NSUM = 256
NB_OUT = 4
NE = 16
NGRID = 256
PAIRS = 1024


def plant(result, stream_key, smallest, top_value):
    spot = [jax.random.randint(jax.random.fold_in(stream_key, axis), (), 0, length) for axis, length in enumerate(result.shape)]
    widest = result.shape.index(max(result.shape))
    beside = spot[:widest] + [(spot[widest] + 1) % result.shape[widest]] + spot[widest + 1:]
    return result.at[tuple(spot)].set(smallest).at[tuple(beside)].set(top_value)


def shard_levels(rng, shape, split, least, high):
    def one(axis_at, blocks):
        heights = jax.random.uniform(jax.random.fold_in(jax.random.fold_in(rng, 6), axis_at), (blocks,), jnp.float32, least / len(split), high / len(split))
        return jnp.repeat(jnp.exp(heights), shape[axis_at] // blocks).reshape((-1,) + (1,) * (len(shape) - axis_at - 1))

    loudness = one(*split[0])
    for cut in split[1:]:
        loudness = loudness * one(*cut)
    return loudness


def gaussian(own_key, extent, deviation, limit, pieces=(), kind=jnp.bfloat16):
    entries = jax.random.normal(own_key, extent, jnp.float32) * deviation
    if len(pieces) > 0:
        entries = shard_levels(own_key, extent, pieces, -0.22, 0.18) * entries
    return jnp.clip(entries, min=-limit, max=limit).astype(kind)


def setup_inputs(seed: int = 0) -> dict:
    key_list = jax.random.split(jax.random.key(seed), 6)
    screened = gaussian(key_list[0], (2, NG, NG), 1.0, 6.0, ((1, 4), (2, 8)))
    elements = gaussian(key_list[1], (2, PAIRS, NG), NG ** -0.5, 0.046875, ((2, 32),))
    energy_grid = jnp.clip(jax.random.uniform(key_list[2], (NGRID,), jnp.float32, -3.0, 3.0), -3.0, 3.0)
    band_index = plant(jax.random.randint(key_list[3], (NSUM,), 0, NGRID), jax.random.fold_in(key_list[3], 1), 0, NGRID - 1).astype(jnp.int32)
    energy_index = plant(jax.random.randint(key_list[4], (NB_OUT, NE), 0, NGRID), jax.random.fold_in(key_list[4], 1), 0, NGRID - 1).astype(jnp.int32)
    return {"screened": screened, "elements": elements, "energy_grid": energy_grid, "band_index": band_index, "energy_index": energy_index}


def weights(energy_grid, band_index, energy_index):
    band_energy = jnp.take(energy_grid, band_index)
    eval_energy = jnp.take(energy_grid, energy_index)
    offset = eval_energy[:, None, :] - band_energy[None, :, None]
    denom = offset * offset + 0.25
    return offset / denom, -0.5 / denom


def reference(screened, elements, energy_grid, band_index, energy_index):
    blocks = 8
    size = NG // blocks
    mats = elements.astype(jnp.float32)

    def step(carry, block):
        wblock = lax.dynamic_slice_in_dim(screened, block * size, size, 1).astype(jnp.float32)
        mblock = lax.dynamic_slice_in_dim(mats, block * size, size, 2)
        prod = jnp.einsum("mph,wgh->mpwg", mats, wblock)
        yre = prod[0, :, 0] - prod[1, :, 1]
        yim = prod[1, :, 0] + prod[0, :, 1]
        sre = jnp.sum(mblock[0] * yre + mblock[1] * yim, axis=-1)
        sim = jnp.sum(mblock[0] * yim - mblock[1] * yre, axis=-1)
        return (carry[0] + sre, carry[1] + sim), None

    zero = jnp.zeros((PAIRS,), jnp.float32)
    (s_re, s_im), _ = lax.scan(step, (zero, zero), jnp.arange(blocks, dtype=jnp.int32))
    wre, wim = weights(energy_grid, band_index, energy_index)
    sre = s_re.reshape(NB_OUT, NSUM)[:, :, None]
    sim = s_im.reshape(NB_OUT, NSUM)[:, :, None]
    scale = NSUM ** -0.5
    out_re = scale * jnp.sum(wre * sre - wim * sim, axis=1)
    out_im = scale * jnp.sum(wre * sim + wim * sre, axis=1)
    return jnp.stack([out_re, out_im])
```

```python
import functools

import jax
import jax.numpy as jnp
from jax import lax
from jax.experimental import pallas as pl
from jax.experimental.pallas import tpu as pltpu
from jax.sharding import PartitionSpec as P

MESH = pl.DeviceIdType.MESH
CHUNKS = 4
TILE = 512


def kernel(
    ngrow, ngcol, w_ref, e_ref, grid_ref, band_ref, eidx_ref, out_ref,
    rows, cols, acc, wbuf, svec, tiles, mine,
    up_sem, dn_sem, pt_sem, lay_sem, row_sem, col_sem, loc_sem, own_sem, w_sem, t_send, t_recv,
):
    nq = ngcol // 2
    held = nq
    pairs = e_ref.shape[1]
    depth = e_ref.shape[2]
    width = w_ref.shape[2]
    chunk = pairs // CHUNKS
    r = lax.axis_index("grow")
    c = lax.axis_index("gcol")
    q = c // 2
    k = c % 2
    mate = 2 * q + 1 - k

    def swap(v):
        return v + (v // 2 % 2) * (1 - 2 * (v % 2))

    pos = swap(r)
    source = q
    after = swap(lax.rem(pos + 1, ngrow))
    before = swap(lax.rem(pos + ngrow - 1, ngrow))
    dist = lax.rem(pos - swap(source) + ngrow, ngrow)
    is_source = dist == 0

    near = jnp.minimum(q, nq - 1 - q)

    def order(t):
        alternate = jnp.where(t % 2 == 1, q - (t + 1) // 2, q + t // 2)
        rest = jnp.where(q > near, q - (t - near), q + (t - near))
        return jnp.where(t <= 2 * near, alternate, rest)

    barrier = pltpu.get_barrier_semaphore()
    for step in range(1, ngcol):
        pl.semaphore_signal(
            barrier, inc=1, device_id=(r, lax.rem(c + step, ngcol)), device_id_type=MESH
        )
    for step in range(1, ngrow):
        pl.semaphore_signal(
            barrier, inc=1, device_id=(lax.rem(r + step, ngrow), c), device_id_type=MESH
        )

    own = pltpu.make_async_copy(e_ref, rows.at[c], own_sem)
    own.start()
    pl.semaphore_wait(barrier, ngcol + ngrow - 2)

    def span(i):
        return pl.ds(pl.multiple_of(i * chunk, chunk), chunk)

    def send(src, slot, i, sem, target):
        return pltpu.make_async_remote_copy(
            src_ref=src, dst_ref=rows.at[slot, :, span(i), :], send_sem=sem,
            recv_sem=row_sem.at[slot, i], device_id=(r, target), device_id_type=MESH,
        )

    def from_own(i, sems, target):
        return send(e_ref.at[:, span(i), :], c, i, sems.at[q, i], target)

    def from_rows(qt, i, sems, target):
        slot = 2 * qt + k
        return send(rows.at[slot, :, span(i), :], slot, i, sems.at[qt, i], target)

    for i in range(CHUNKS):
        @pl.when(q + 1 < nq)
        def _():
            from_own(i, up_sem, c + 2).start()

        @pl.when(q >= 1)
        def _():
            from_own(i, dn_sem, c - 2).start()

        from_own(i, pt_sem, mate).start()

    def w_copy(qt):
        block = pl.ds(pl.multiple_of(qt * 2 * depth, 2 * depth), 2 * depth)
        return pltpu.make_async_copy(w_ref.at[:, block, :], wbuf, w_sem)

    acc[...] = jnp.zeros_like(acc)

    def spread_copy(src, slot, i, part, target):
        return pltpu.make_async_remote_copy(
            src_ref=src, dst_ref=cols.at[slot, part, span(i), :], send_sem=lay_sem.at[slot, i, part],
            recv_sem=col_sem.at[slot, i, part], device_id=(target, c), device_id_type=MESH,
        )

    def place_copy(qt, b, i):
        return pltpu.make_async_copy(
            rows.at[2 * qt + b, :, span(i), :],
            cols.at[2 * qt + b - k * held, :, span(i), :],
            loc_sem.at[2 * qt + b - k * held, i],
        )

    def mine_half(qt):
        return qt // (nq // 2) == k

    steps = nq * CHUNKS

    def tick(tau, carry):
        @pl.when(tau < steps)
        def _():
            t = tau // CHUNKS
            i = tau % CHUNKS
            qt = order(t)

            @pl.when(i == 0)
            def _():
                w_copy(qt).start()

            @pl.when(tau == 0)
            def _():
                pltpu.make_async_copy(e_ref, rows.at[c], own_sem).wait()

            @pl.when(t > 0)
            def _():
                from_rows(qt, i, pt_sem, mate).wait_recv()

                @pl.when(jnp.logical_and(qt < q, q + 1 < nq))
                def _():
                    from_rows(qt, i, up_sem, c + 2).start()

                @pl.when(jnp.logical_and(qt > q, q >= 1))
                def _():
                    from_rows(qt, i, dn_sem, c - 2).start()

                from_rows(qt, i, pt_sem, mate).start()

            other = 2 * qt + 1 - k
            send(rows.at[other, :, span(i), :], other, i, pt_sem.at[qt, i], mate).wait_recv()

            @pl.when(jnp.logical_and(is_source, mine_half(qt)))
            def _():
                for b in range(2):
                    slot = 2 * qt + b - k * held
                    whole = rows.at[2 * qt + b]
                    spread_copy(whole.at[0, span(i), :], slot, i, 0, after).start()
                    spread_copy(whole.at[1, span(i), :], slot, i, 1, before).start()
                    place_copy(qt, b, i).start()

            @pl.when(i == 0)
            def _():
                w_copy(qt).wait()

            def column(n, carry):
                lanes = pl.ds(pl.multiple_of(n * TILE, TILE), TILE)
                dot = functools.partial(jnp.dot, preferred_element_type=jnp.float32)
                re = acc[0, span(i), lanes]
                im = acc[1, span(i), lanes]
                for b in range(2):
                    mre = rows[2 * qt + b, 0, span(i), :]
                    mim = rows[2 * qt + b, 1, span(i), :]
                    wre = wbuf[0, b * depth:(b + 1) * depth, lanes]
                    wim = wbuf[1, b * depth:(b + 1) * depth, lanes]
                    re += dot(mre, wre) + dot(mim, wim)
                    im += dot(mre, wim) + dot(mim, -wre)
                acc[0, span(i), lanes] = re
                acc[1, span(i), lanes] = im
                return carry

            lax.fori_loop(0, width // TILE, column, 0)

        for part in range(2):
            hops = dist if part == 0 else lax.rem(ngrow - dist, ngrow)
            past = tau - hops

            @pl.when(jnp.logical_and(hops > 0, jnp.logical_and(past >= 0, past < steps)))
            def _():
                t = past // CHUNKS
                i = past % CHUNKS
                qt = order(t)

                @pl.when(mine_half(qt))
                def _():
                    for b in range(2):
                        slot = 2 * qt + b - k * held
                        onward = spread_copy(
                            cols.at[slot, part, span(i), :], slot, i, part,
                            after if part == 0 else before,
                        )
                        onward.wait_recv()

                        @pl.when(hops < ngrow - 1)
                        def _():
                            onward.start()

        return carry

    lax.fori_loop(0, steps + ngrow - 1, tick, 0)

    @pl.when(is_source)
    def _():
        for slot in range(held):
            for i in range(CHUNKS):
                pltpu.make_async_copy(
                    rows.at[k * held + slot, :, span(i), :], cols.at[slot, :, span(i), :],
                    loc_sem.at[slot, i],
                ).wait()

    band = 64

    def contract(p, carry):
        here = pl.ds(pl.multiple_of(p * band, band), band)
        s_re = jnp.zeros((band, 1), jnp.float32)
        s_im = jnp.zeros((band, 1), jnp.float32)
        for slot in range(held):
            lanes = slice(slot * depth, (slot + 1) * depth)
            zre = acc[0, here, lanes]
            zim = acc[1, here, lanes]
            mre = cols[slot, 0, here, :].astype(jnp.float32)
            mim = cols[slot, 1, here, :].astype(jnp.float32)
            s_re += jnp.sum(zre * mre - zim * mim, axis=1, keepdims=True)
            s_im += jnp.sum(zre * mim + zim * mre, axis=1, keepdims=True)
        svec[0, here, :] = s_re
        svec[1, here, :] = s_im
        return carry

    lax.fori_loop(0, pairs // band, contract, 0)

    nb, ne = eidx_ref.shape
    summed = band_ref.shape[1]
    npoint = grid_ref.shape[1]
    energy = grid_ref[...]

    def iota(shape, dim):
        return lax.broadcasted_iota(jnp.int32, shape, dim)

    square = (npoint, npoint)
    energy_col = jnp.sum(jnp.where(iota(square, 0) == iota(square, 1), energy, 0.0), axis=1, keepdims=True)
    diag = (summed, summed)
    index_col = jnp.sum(
        jnp.where(iota(diag, 0) == iota(diag, 1), band_ref[...].astype(jnp.float32), 0.0),
        axis=1, keepdims=True,
    )
    points = iota((summed, npoint), 1).astype(jnp.float32)
    band_energy = jnp.sum(jnp.where(index_col == points, energy, 0.0), axis=1, keepdims=True)
    scale = summed ** (-0.5)
    mine[...] = jnp.zeros_like(mine)
    for n in range(nb):
        chosen = iota((npoint, ne), 0) == eidx_ref[n:n + 1, :]
        eval_energy = jnp.sum(jnp.where(chosen, energy_col, 0.0), axis=0, keepdims=True)
        offset = eval_energy - band_energy
        denom = offset * offset + 0.25
        wre = offset / denom
        wim = -0.5 / denom
        sre = svec[0, n * summed:(n + 1) * summed, :]
        sim = svec[1, n * summed:(n + 1) * summed, :]
        mine[n:n + 1, 0:ne] = scale * jnp.sum(wre * sre - wim * sim, axis=0, keepdims=True)
        mine[nb + n:nb + n + 1, 0:ne] = scale * jnp.sum(wre * sim + wim * sre, axis=0, keepdims=True)

    def exchange(base, count, me, device):
        tiles[base + me] = mine[...]

        def to(step):
            return pltpu.make_async_remote_copy(
                src_ref=mine, dst_ref=tiles.at[base + me], send_sem=t_send.at[base + step],
                recv_sem=t_recv.at[base + me], device_id=device(lax.rem(me + step, count)),
                device_id_type=MESH,
            )

        for step in range(1, count):
            to(step).start()
        for step in range(1, count):
            peer = lax.rem(me + step, count)
            pltpu.make_async_remote_copy(
                src_ref=mine, dst_ref=tiles.at[base + peer], send_sem=t_send.at[base + step],
                recv_sem=t_recv.at[base + peer], device_id=device(peer), device_id_type=MESH,
            ).wait_recv()
        for step in range(1, count):
            to(step).wait_send()
        total = tiles[base]
        for j in range(1, count):
            total += tiles[base + j]
        return total

    mine[...] = exchange(0, ngcol, c, lambda v: (r, v))
    total = exchange(ngcol, ngrow, r, lambda v: (v, c))
    out_ref[0] = total[0:nb, 0:ne]
    out_ref[1] = total[nb:2 * nb, 0:ne]

    def drain(j, carry):
        qt = j // CHUNKS
        i = j % CHUNKS

        @pl.when(jnp.logical_and(qt <= q, q + 1 < nq))
        def _():
            from_rows(qt, i, up_sem, c + 2).wait_send()

        @pl.when(jnp.logical_and(qt >= q, q >= 1))
        def _():
            from_rows(qt, i, dn_sem, c - 2).wait_send()

        from_rows(qt, i, pt_sem, mate).wait_send()
        for part in range(2):
            hops = dist if part == 0 else lax.rem(ngrow - dist, ngrow)

            @pl.when(hops < ngrow - 1)
            def _():
                spread_copy(
                    cols.at[qt, part, span(i), :], qt, i, part, after if part == 0 else before
                ).wait_send()

        return carry

    lax.fori_loop(0, nq * CHUNKS, drain, 0)


def solution(mesh):
    ngrow = mesh.shape["grow"]
    ngcol = mesh.shape["gcol"]
    nq = ngcol // 2

    def local(screened, elements, energy_grid, band_index, energy_index):
        _, pairs, depth = elements.shape
        width = screened.shape[2]
        nb, ne = energy_index.shape
        dma = pltpu.SemaphoreType.DMA
        vmem = pl.BlockSpec(memory_space=pltpu.VMEM)
        hbm = pl.BlockSpec(memory_space=pl.ANY)
        return pl.pallas_call(
            functools.partial(kernel, ngrow, ngcol),
            out_shape=jax.ShapeDtypeStruct((2, nb, ne), jnp.float32),
            in_specs=[hbm, hbm, vmem, vmem, vmem],
            out_specs=vmem,
            scratch_shapes=[
                pltpu.VMEM((ngcol, 2, pairs, depth), jnp.bfloat16),
                pltpu.VMEM((nq, 2, pairs, depth), jnp.bfloat16),
                pltpu.VMEM((2, pairs, width), jnp.float32),
                pltpu.VMEM((2, 2 * depth, width), jnp.bfloat16),
                pltpu.VMEM((2, pairs, 1), jnp.float32),
                pltpu.VMEM((ngcol + ngrow, 2 * nb, 128), jnp.float32),
                pltpu.VMEM((2 * nb, 128), jnp.float32),
                dma((nq, CHUNKS)),
                dma((nq, CHUNKS)),
                dma((nq, CHUNKS)),
                dma((nq, CHUNKS, 2)),
                dma((ngcol, CHUNKS)),
                dma((nq, CHUNKS, 2)),
                dma((nq, CHUNKS)),
                dma,
                dma,
                dma((ngcol + ngrow,)),
                dma((ngcol + ngrow,)),
            ],
            compiler_params=pltpu.CompilerParams(
                collective_id=0, has_side_effects=True, vmem_limit_bytes=60 * 1024 * 1024
            ),
            cost_estimate=pl.CostEstimate(
                flops=8 * pairs * screened.shape[1] * width,
                bytes_accessed=screened.size * 2, transcendentals=0,
            ),
        )(screened, elements, energy_grid[None], band_index[None], energy_index)

    in_specs = (P(None, "grow", "gcol"), P(None, None, ("grow", "gcol")), P(), P(), P())
    return jax.shard_map(local, mesh=mesh, in_specs=in_specs, out_specs=P(), check_vma=False)
```

```python
import functools

import jax
import jax.numpy as jnp
from jax import lax
from jax.experimental import pallas as pl
from jax.experimental.pallas import tpu as pltpu
from jax.sharding import PartitionSpec as P

MESH = pl.DeviceIdType.MESH
CHUNKS = 8
TILE = 512


def kernel(
    ngrow, ngcol, w_ref, e_ref, grid_ref, band_ref, eidx_ref, out_ref,
    rows, cols, acc, wbuf, svec, tiles, mine,
    up_sem, dn_sem, pt_sem, lay_sem, row_sem, col_sem, loc_sem, own_sem, w_sem, t_send, t_recv,
):
    nq = ngcol // 2
    held = nq
    pairs = e_ref.shape[1]
    depth = e_ref.shape[2]
    width = w_ref.shape[2]
    chunk = pairs // CHUNKS
    r = lax.axis_index("grow")
    c = lax.axis_index("gcol")
    q = c // 2
    k = c % 2
    mate = 2 * q + 1 - k

    def swap(v):
        return v + (v // 2 % 2) * (1 - 2 * (v % 2))

    pos = swap(r)
    source = q
    after = swap(lax.rem(pos + 1, ngrow))
    before = swap(lax.rem(pos + ngrow - 1, ngrow))
    dist = lax.rem(pos - swap(source) + ngrow, ngrow)
    is_source = dist == 0

    near = jnp.minimum(q, nq - 1 - q)

    def order(t):
        ahead = jnp.where(q > near, -1, 1)
        alternate = jnp.where(t % 2 == 1, q + ahead * ((t + 1) // 2), q - ahead * (t // 2))
        rest = jnp.where(q > near, q - (t - near), q + (t - near))
        return jnp.where(t <= 2 * near, alternate, rest)

    barrier = pltpu.get_barrier_semaphore()
    for step in range(1, ngcol):
        pl.semaphore_signal(
            barrier, inc=1, device_id=(r, lax.rem(c + step, ngcol)), device_id_type=MESH
        )
    for step in range(1, ngrow):
        pl.semaphore_signal(
            barrier, inc=1, device_id=(lax.rem(r + step, ngrow), c), device_id_type=MESH
        )

    own = pltpu.make_async_copy(e_ref, rows.at[c], own_sem)
    own.start()
    pl.semaphore_wait(barrier, ngcol + ngrow - 2)

    def span(i):
        return pl.ds(pl.multiple_of(i * chunk, chunk), chunk)

    def send(src, slot, i, sem, target):
        return pltpu.make_async_remote_copy(
            src_ref=src, dst_ref=rows.at[slot, :, span(i), :], send_sem=sem,
            recv_sem=row_sem.at[slot, i], device_id=(r, target), device_id_type=MESH,
        )

    def from_own(i, sems, target):
        return send(e_ref.at[:, span(i), :], c, i, sems.at[q, i], target)

    def from_rows(qt, i, sems, target):
        slot = 2 * qt + k
        return send(rows.at[slot, :, span(i), :], slot, i, sems.at[qt, i], target)

    for i in range(CHUNKS):
        @pl.when(q + 1 < nq)
        def _():
            from_own(i, up_sem, c + 2).start()

        @pl.when(q >= 1)
        def _():
            from_own(i, dn_sem, c - 2).start()

        from_own(i, pt_sem, mate).start()

    def w_copy(qt):
        block = pl.ds(pl.multiple_of(qt * 2 * depth, 2 * depth), 2 * depth)
        return pltpu.make_async_copy(w_ref.at[:, block, :], wbuf, w_sem)

    acc[...] = jnp.zeros_like(acc)

    def spread_copy(src, slot, i, part, target):
        return pltpu.make_async_remote_copy(
            src_ref=src, dst_ref=cols.at[slot, part, span(i), :], send_sem=lay_sem.at[slot, i, part],
            recv_sem=col_sem.at[slot, i, part], device_id=(target, c), device_id_type=MESH,
        )

    def place_copy(qt, b, i):
        return pltpu.make_async_copy(
            rows.at[2 * qt + b, :, span(i), :],
            cols.at[2 * qt + b - k * held, :, span(i), :],
            loc_sem.at[2 * qt + b - k * held, i],
        )

    def mine_half(qt):
        return qt // (nq // 2) == k

    steps = nq * CHUNKS

    band = 64

    def contract(p, carry):
        here = pl.ds(pl.multiple_of(p * band, band), band)
        s_re = jnp.zeros((band, 1), jnp.float32)
        s_im = jnp.zeros((band, 1), jnp.float32)
        for slot in range(held):
            lanes = slice(slot * depth, (slot + 1) * depth)
            zre = acc[0, here, lanes]
            zim = acc[1, here, lanes]
            mre = cols[slot, 0, here, :].astype(jnp.float32)
            mim = cols[slot, 1, here, :].astype(jnp.float32)
            s_re += jnp.sum(zre * mre - zim * mim, axis=1, keepdims=True)
            s_im += jnp.sum(zre * mim + zim * mre, axis=1, keepdims=True)
        svec[0, here, :] = s_re
        svec[1, here, :] = s_im
        return carry

    def tick(tau, carry):
        @pl.when(tau < steps)
        def _():
            t = tau // CHUNKS
            i = tau % CHUNKS
            qt = order(t)

            @pl.when(i == 0)
            def _():
                w_copy(qt).start()

            @pl.when(tau == 0)
            def _():
                pltpu.make_async_copy(e_ref, rows.at[c], own_sem).wait()

            @pl.when(t > 0)
            def _():
                from_rows(qt, i, pt_sem, mate).wait_recv()

                @pl.when(jnp.logical_and(qt < q, q + 1 < nq))
                def _():
                    from_rows(qt, i, up_sem, c + 2).start()

                @pl.when(jnp.logical_and(qt > q, q >= 1))
                def _():
                    from_rows(qt, i, dn_sem, c - 2).start()

                from_rows(qt, i, pt_sem, mate).start()

            other = 2 * qt + 1 - k
            send(rows.at[other, :, span(i), :], other, i, pt_sem.at[qt, i], mate).wait_recv()

            @pl.when(jnp.logical_and(is_source, mine_half(qt)))
            def _():
                for b in range(2):
                    slot = 2 * qt + b - k * held
                    whole = rows.at[2 * qt + b]
                    spread_copy(whole.at[0, span(i), :], slot, i, 0, after).start()
                    spread_copy(whole.at[1, span(i), :], slot, i, 1, before).start()
                    place_copy(qt, b, i).start()

        for part in range(2):
            hops = dist if part == 0 else lax.rem(ngrow - dist, ngrow)
            past = tau - hops

            @pl.when(jnp.logical_and(hops > 0, jnp.logical_and(past >= 0, past < steps)))
            def _():
                t = past // CHUNKS
                i = past % CHUNKS
                qt = order(t)

                @pl.when(mine_half(qt))
                def _():
                    for b in range(2):
                        slot = 2 * qt + b - k * held
                        onward = spread_copy(
                            cols.at[slot, part, span(i), :], slot, i, part,
                            after if part == 0 else before,
                        )
                        onward.wait_recv()

                        @pl.when(hops < ngrow - 1)
                        def _():
                            onward.start()

        @pl.when(tau < steps)
        def _():
            t = tau // CHUNKS
            i = tau % CHUNKS
            qt = order(t)

            def multiply(first, size):
                here = pl.ds(pl.multiple_of(first, size), size)

                def column(n, carry):
                    lanes = pl.ds(pl.multiple_of(n * TILE, TILE), TILE)
                    dot = functools.partial(jnp.dot, preferred_element_type=jnp.float32)
                    re = acc[0, here, lanes]
                    im = acc[1, here, lanes]
                    for b in range(2):
                        mre = rows[2 * qt + b, 0, here, :]
                        mim = rows[2 * qt + b, 1, here, :]
                        wre = wbuf[0, b * depth:(b + 1) * depth, lanes]
                        wim = wbuf[1, b * depth:(b + 1) * depth, lanes]
                        re += dot(mre, wre) + dot(mim, wim)
                        im += dot(mre, wim) + dot(mim, -wre)
                    acc[0, here, lanes] = re
                    acc[1, here, lanes] = im
                    return carry

                lax.fori_loop(0, width // TILE, column, 0)

            @pl.when(i == 1)
            def _():
                @pl.when(t < nq - 1)
                def _():
                    w_copy(qt).wait()

            @pl.when(jnp.logical_and(i == 0, t == nq - 1))
            def _():
                w_copy(qt).wait()

            @pl.when(jnp.logical_and(i % 2 == 1, t < nq - 1))
            def _():
                multiply((i - 1) * chunk, 2 * chunk)

            @pl.when(t == nq - 1)
            def _():
                multiply(i * chunk, chunk)

        done = tau - (steps - CHUNKS) - (ngrow - 1)

        @pl.when(done >= 0)
        def _():
            @pl.when(is_source)
            def _():
                for slot in range(held):
                    pltpu.make_async_copy(
                        rows.at[k * held + slot, :, span(done), :], cols.at[slot, :, span(done), :],
                        loc_sem.at[slot, done],
                    ).wait()

            lax.fori_loop(done * (chunk // band), (done + 1) * (chunk // band), contract, 0)

        return carry

    lax.fori_loop(0, steps + ngrow - 1, tick, 0)

    nb, ne = eidx_ref.shape
    summed = band_ref.shape[1]
    npoint = grid_ref.shape[1]
    energy = grid_ref[...]

    def iota(shape, dim):
        return lax.broadcasted_iota(jnp.int32, shape, dim)

    square = (npoint, npoint)
    energy_col = jnp.sum(jnp.where(iota(square, 0) == iota(square, 1), energy, 0.0), axis=1, keepdims=True)
    diag = (summed, summed)
    index_col = jnp.sum(
        jnp.where(iota(diag, 0) == iota(diag, 1), band_ref[...].astype(jnp.float32), 0.0),
        axis=1, keepdims=True,
    )
    points = iota((summed, npoint), 1).astype(jnp.float32)
    band_energy = jnp.sum(jnp.where(index_col == points, energy, 0.0), axis=1, keepdims=True)
    scale = summed ** (-0.5)
    mine[...] = jnp.zeros_like(mine)
    for n in range(nb):
        chosen = iota((npoint, ne), 0) == eidx_ref[n:n + 1, :]
        eval_energy = jnp.sum(jnp.where(chosen, energy_col, 0.0), axis=0, keepdims=True)
        offset = eval_energy - band_energy
        denom = offset * offset + 0.25
        wre = offset / denom
        wim = -0.5 / denom
        sre = svec[0, n * summed:(n + 1) * summed, :]
        sim = svec[1, n * summed:(n + 1) * summed, :]
        mine[n:n + 1, 0:ne] = scale * jnp.sum(wre * sre - wim * sim, axis=0, keepdims=True)
        mine[nb + n:nb + n + 1, 0:ne] = scale * jnp.sum(wre * sim + wim * sre, axis=0, keepdims=True)

    def exchange(base, count, me, device):
        tiles[base + me] = mine[...]

        def to(step):
            return pltpu.make_async_remote_copy(
                src_ref=mine, dst_ref=tiles.at[base + me], send_sem=t_send.at[base + step],
                recv_sem=t_recv.at[base + me], device_id=device(lax.rem(me + step, count)),
                device_id_type=MESH,
            )

        for step in range(1, count):
            to(step).start()
        for step in range(1, count):
            peer = lax.rem(me + step, count)
            pltpu.make_async_remote_copy(
                src_ref=mine, dst_ref=tiles.at[base + peer], send_sem=t_send.at[base + step],
                recv_sem=t_recv.at[base + peer], device_id=device(peer), device_id_type=MESH,
            ).wait_recv()
        for step in range(1, count):
            to(step).wait_send()
        total = tiles[base]
        for j in range(1, count):
            total += tiles[base + j]
        return total

    mine[...] = exchange(0, ngcol, c, lambda v: (r, v))
    total = exchange(ngcol, ngrow, r, lambda v: (v, c))
    out_ref[0] = total[0:nb, 0:ne]
    out_ref[1] = total[nb:2 * nb, 0:ne]

    def drain(j, carry):
        qt = j // CHUNKS
        i = j % CHUNKS

        @pl.when(jnp.logical_and(qt <= q, q + 1 < nq))
        def _():
            from_rows(qt, i, up_sem, c + 2).wait_send()

        @pl.when(jnp.logical_and(qt >= q, q >= 1))
        def _():
            from_rows(qt, i, dn_sem, c - 2).wait_send()

        from_rows(qt, i, pt_sem, mate).wait_send()
        for part in range(2):
            hops = dist if part == 0 else lax.rem(ngrow - dist, ngrow)

            @pl.when(hops < ngrow - 1)
            def _():
                spread_copy(
                    cols.at[qt, part, span(i), :], qt, i, part, after if part == 0 else before
                ).wait_send()

        return carry

    lax.fori_loop(0, nq * CHUNKS, drain, 0)


def solution(mesh):
    ngrow = mesh.shape["grow"]
    ngcol = mesh.shape["gcol"]
    nq = ngcol // 2

    def local(screened, elements, energy_grid, band_index, energy_index):
        _, pairs, depth = elements.shape
        width = screened.shape[2]
        nb, ne = energy_index.shape
        dma = pltpu.SemaphoreType.DMA
        vmem = pl.BlockSpec(memory_space=pltpu.VMEM)
        hbm = pl.BlockSpec(memory_space=pl.ANY)
        return pl.pallas_call(
            functools.partial(kernel, ngrow, ngcol),
            out_shape=jax.ShapeDtypeStruct((2, nb, ne), jnp.float32),
            in_specs=[hbm, hbm, vmem, vmem, vmem],
            out_specs=vmem,
            scratch_shapes=[
                pltpu.VMEM((ngcol, 2, pairs, depth), jnp.bfloat16),
                pltpu.VMEM((nq, 2, pairs, depth), jnp.bfloat16),
                pltpu.VMEM((2, pairs, width), jnp.float32),
                pltpu.VMEM((2, 2 * depth, width), jnp.bfloat16),
                pltpu.VMEM((2, pairs, 1), jnp.float32),
                pltpu.VMEM((ngcol + ngrow, 2 * nb, 128), jnp.float32),
                pltpu.VMEM((2 * nb, 128), jnp.float32),
                dma((nq, CHUNKS)),
                dma((nq, CHUNKS)),
                dma((nq, CHUNKS)),
                dma((nq, CHUNKS, 2)),
                dma((ngcol, CHUNKS)),
                dma((nq, CHUNKS, 2)),
                dma((nq, CHUNKS)),
                dma,
                dma,
                dma((ngcol + ngrow,)),
                dma((ngcol + ngrow,)),
            ],
            compiler_params=pltpu.CompilerParams(
                collective_id=0, has_side_effects=True, vmem_limit_bytes=60 * 1024 * 1024
            ),
            cost_estimate=pl.CostEstimate(
                flops=8 * pairs * screened.shape[1] * width,
                bytes_accessed=screened.size * 2, transcendentals=0,
            ),
        )(screened, elements, energy_grid[None], band_index[None], energy_index)

    in_specs = (P(None, "grow", "gcol"), P(None, None, ("grow", "gcol")), P(), P(), P())
    return jax.shard_map(local, mesh=mesh, in_specs=in_specs, out_specs=P(), check_vma=False)
```
